32 devices in a mesh: ex: 16 (over z, y, core), grp: 2 (over x).
Axes of the slice: x: 2, y: 2, z: 4, core: 2. Of those that a mesh axis runs over, the one named last changes fastest.
Arguments:
- queries: bfloat16 [4096, 65536], P('ex', 'grp'), may hold values from -6 to 6
- inv_in: bfloat16 [16, 64, 64], P('grp'), as said below
- inv_out: bfloat16 [16, 64, 64], P('grp'), as said below
- store: bfloat16 [8192, 65536], P('ex', 'grp'), may hold values from -0.0234375 to 0.0234375
- listed: int32 [128, 24], P('ex'), may hold values from 0 to 1, as said below
Outputs:
- scores: float32 [3, 4096, 512], P(None, ('ex', 'grp'))
The draws below stay inside these ranges and needn't reach their ends.
Inputs may be any that keep to these rules, and one draw needn't show every extreme that they name: Entries are 0 or 1; every query block lists column 0 and column 23, the other numbers listed differ from block to block and from ex block to ex block, and some query block lists all 24. `inv_in`: each matrix is symmetric and positive definite. `inv_out`: each matrix is symmetric and positive definite.
All inputs are finite; a program needn't handle non-finite values.
Results may differ from the reference program's by a relative error of at most 0.0041.
Values may be sent and summed in bfloat16 or wider, within the bound.
No kernel may reach another device: no remote copies, remote signals or barrier semaphores. Data moves between devices by JAX's collectives and lax.ppermute only.
A program may use at most 192 MiB of HBM per device.

```python
import jax
import jax.numpy as jnp
from jax import lax

R = 64
MODULES = 16
QB = 32
SUB = 64
QRY_DEV = 256
EX_DEV = 512
GD = 65536
SB = 8
QUERIES = 4096
EXAMPLES = 8192
NQB = 128
N_EX = 16


def factor_draw(key):
    base = jax.random.normal(key, (MODULES, R, R), jnp.float32)
    outer = jnp.einsum('mab,mcb->mac', base, base) / R
    return 0.6 * jnp.eye(R, dtype=jnp.float32)[None] + 0.4 * outer


def draw_inv_in(key, part):
    return factor_draw(jax.random.fold_in(key, 11)).astype(jnp.bfloat16)


def draw_inv_out(key, part):
    return factor_draw(jax.random.fold_in(key, 23)).astype(jnp.bfloat16)


def draw_listed(key, part):
    key = jax.random.fold_in(key, 37)
    first, second, third = jax.random.split(key, 3)
    width = 3 * SB
    per_dev = QRY_DEV // QB
    level = jax.random.randint(first, (NQB // per_dev,), 0, width)
    device_level = jnp.repeat(level, per_dev)
    extra = jax.random.randint(second, (NQB,), 0, width)
    counts = jnp.maximum(2, 1 + jnp.minimum(width - 1, (device_level * 3 + extra) // 4))
    counts = counts.at[0].set(width)
    column = jnp.arange(width, dtype=jnp.int32)[None, :]
    scores_int = jax.random.randint(third, (NQB, width), 0, 1 << 20) * width + column
    scores_int = jnp.where(column == 0, -2, jnp.where(column == width - 1, -1, scores_int))
    rank = jnp.argsort(jnp.argsort(scores_int, axis=1), axis=1)
    return (rank < counts[:, None]).astype(jnp.int32)


def block_scale(key, shape, shards, low, top_value):
    def one(position, blocks):
        draws = jax.random.uniform(jax.random.fold_in(jax.random.fold_in(key, 6), position), (blocks,), jnp.float32, low / len(shards), top_value / len(shards))
        return jnp.repeat(jnp.exp(draws), shape[position] // blocks).reshape((-1,) + (1,) * (len(shape) - position - 1))

    factor_of = one(*shards[0])
    for cut in shards[1:]:
        factor_of = factor_of * one(*cut)
    return factor_of


def gaussian(rng, dims, deviation, bound, shards=(), held_as=jnp.bfloat16):
    array = jax.random.normal(rng, dims, jnp.float32) * deviation
    if len(shards) > 0:
        array = block_scale(rng, dims, shards, -0.22, 0.18) * array
    return jnp.clip(array, min=-bound, max=bound).astype(held_as)


def setup_inputs(seed: int = 0) -> dict:
    seeds = jax.random.split(jax.random.key(seed), 6)
    return {
        "queries": gaussian(seeds[0], (QUERIES, GD), 1.0, 6.0, ((0, 16), (1, 2))),
        "inv_in": draw_inv_in(jax.random.fold_in(seeds[5], 71), 0),
        "inv_out": draw_inv_out(jax.random.fold_in(seeds[5], 71), 0),
        "store": gaussian(seeds[3], (EXAMPLES, GD), GD ** -0.5, 0.0234375, ((0, 16), (1, 2))),
        "listed": draw_listed(jax.random.fold_in(seeds[5], 71), 0),
    }


def widen(piece):
    count = piece.shape[1]
    rows = piece.shape[0]
    full = jnp.broadcast_to(piece.astype(jnp.float32)[:, None, :, None], (rows, QB, count, SUB))
    return full.reshape(rows * QB, count * SUB)


def reference(queries, inv_in, inv_out, store, listed):
    inv_left = inv_in.astype(jnp.float32)
    inv_right = inv_out.astype(jnp.float32)

    def one_block(block):
        start = (block * QRY_DEV).astype(jnp.int32)
        query_part = lax.dynamic_slice_in_dim(queries, start, QRY_DEV, 0).astype(jnp.float32)
        query_part = query_part.reshape(QRY_DEV, MODULES, R, R)
        left = jnp.einsum("mab,qmbc->qmac", inv_left, query_part, precision=lax.Precision.HIGHEST)
        left = lax.optimization_barrier(left.astype(jnp.bfloat16)).astype(jnp.float32)
        ready = jnp.einsum("qmac,mcd->qmad", left, inv_right, precision=lax.Precision.HIGHEST)
        ready = ready.reshape(QRY_DEV, GD).astype(jnp.bfloat16)
        listed_rows = lax.dynamic_slice_in_dim(listed, (block * (QRY_DEV // QB)).astype(jnp.int32), QRY_DEV // QB, 0)
        results = []
        for window in range(3):
            source = ((block + window - 1 + N_EX) % N_EX).astype(jnp.int32)
            slab = lax.dynamic_slice_in_dim(store, (source * EX_DEV).astype(jnp.int32), EX_DEV, 0)
            part = lax.dot_general(ready, slab, (((1,), (1,)), ((), ())), preferred_element_type=jnp.float32)
            results.append(part * widen(listed_rows[:, window * SB:(window + 1) * SB]))
        return jnp.stack(results)

    every = lax.map(one_block, jnp.arange(N_EX, dtype=jnp.int32))
    return jnp.transpose(every, (1, 0, 2, 3)).reshape(3, QUERIES, EX_DEV)
```

```python
import functools

import jax
import jax.numpy as jnp
from jax import lax
from jax.experimental import pallas as pl
from jax.experimental.pallas import tpu as pltpu
from jax.sharding import PartitionSpec as P

QB = 32
SUB = 64
CHUNKS = (1, 3, 6, 2, 4)
PIECES = (3, 3, 2)
WIDE = 256
LOW = 8
VMEM = 56 * 1024 * 1024
NT = (((1,), (1,)), ((), ()))
TN = (((0,), (0,)), ((), ()))


def spread(matrix, rows_of, columns_of, keep):
    tall = jnp.dot(rows_of, matrix, preferred_element_type=jnp.float32)
    full = lax.dot_general(
        tall.astype(jnp.bfloat16), columns_of, NT, preferred_element_type=jnp.float32
    )
    return jnp.where(keep, full, 0.0).astype(jnp.bfloat16)


def precondition(x, inv_in, inv_out, turned, left):
    n, size = x.shape
    side = inv_in.shape[0]
    high = side // LOW
    per = WIDE // side

    def iota(shape, dim):
        return lax.broadcasted_iota(jnp.int32, shape, dim)

    def unit(rows, columns, test):
        hit = test(iota((rows, columns), 0), iota((rows, columns), 1))
        return jnp.where(hit, 1.0, 0.0).astype(jnp.bfloat16)

    identity = unit(WIDE, WIDE, lambda r, c: r == c)
    for block in range(size // WIDE):
        part = lax.dot_general(
            identity,
            x[:, block * WIDE : (block + 1) * WIDE],
            NT,
            preferred_element_type=jnp.float32,
        )
        turned[block * per : (block + 1) * per] = part.reshape(per, high, LOW, n)

    span = side * LOW
    expand = unit(span, side, lambda r, c: r // LOW == c)
    square = (span, span)
    factor = spread(inv_in, expand, expand, iota(square, 0) % LOW == iota(square, 1) % LOW)
    for part in range(high):
        piece = turned[:, part].reshape(span, n).astype(jnp.bfloat16)
        result = jnp.dot(factor, piece, preferred_element_type=jnp.float32)
        left[:, part] = result.astype(jnp.bfloat16).astype(jnp.float32).reshape(side, LOW, n)

    repeat = unit(WIDE, side, lambda r, c: r % side == c)
    square = (WIDE, WIDE)
    factor = spread(inv_out, repeat, repeat, iota(square, 0) // side == iota(square, 1) // side)
    blocks = []
    for block in range(size // WIDE):
        piece = left[block * per : (block + 1) * per].reshape(WIDE, n).astype(jnp.bfloat16)
        result = lax.dot_general(piece, factor, TN, preferred_element_type=jnp.float32)
        blocks.append(result.astype(jnp.bfloat16))
    return blocks


def add_scores(rows, slab, out_ref):
    part = lax.dot_general(rows, slab, NT, preferred_element_type=jnp.float32)

    @pl.when(pl.program_id(0) == 0)
    def _():
        out_ref[...] = part.reshape(out_ref.shape)

    @pl.when(pl.program_id(0) != 0)
    def _():
        out_ref[...] += part.reshape(out_ref.shape)


def own_kernel(bounds, x_ref, in_ref, out_ref, slab_ref, *rest):
    chunks, scores_ref, (turned, left, held) = rest[:-4], rest[-4], rest[-3:]
    n = x_ref.shape[0]
    groups = scores_ref.shape[0]
    rows = n // groups
    blocks = precondition(x_ref[...], in_ref[0], out_ref[0], turned, left)
    for index, block in enumerate(blocks):
        cut = pl.ds(index * WIDE, WIDE)
        held[:, cut] = block
        for chunk, low, top in zip(chunks, bounds[:-1], bounds[1:]):
            for group in range(groups):
                chunk[group, :, cut] = block[group * rows + low : group * rows + top]
    add_scores(held[...], slab_ref[...], scores_ref)


def own(queries, inv_in, inv_out, store, groups, bounds):
    n, dims = queries.shape
    modules, side, _ = inv_in.shape
    size = side * side
    examples = store.shape[0]
    small = pl.BlockSpec((1, side, side), lambda m: (m, 0, 0))
    sizes = [top - low for low, top in zip(bounds[:-1], bounds[1:])]
    *chunks, mine = pl.pallas_call(
        functools.partial(own_kernel, bounds),
        grid=(modules,),
        in_specs=[
            pl.BlockSpec((n, size), lambda m: (0, m)),
            small,
            small,
            pl.BlockSpec((examples, size), lambda m: (0, m)),
        ],
        out_specs=[pl.BlockSpec((groups, c, size), lambda m: (0, 0, m)) for c in sizes]
        + [pl.BlockSpec((groups, n // groups, examples), lambda m: (0, 0, 0))],
        out_shape=[jax.ShapeDtypeStruct((groups, c, dims), jnp.bfloat16) for c in sizes]
        + [jax.ShapeDtypeStruct((groups, n // groups, examples), jnp.float32)],
        scratch_shapes=[
            pltpu.VMEM((side, side // LOW, LOW, n), jnp.float32),
            pltpu.VMEM((side, side // LOW, LOW, n), jnp.float32),
            pltpu.VMEM((n, size), jnp.bfloat16),
        ],
        compiler_params=pltpu.CompilerParams(vmem_limit_bytes=VMEM),
        name="own",
    )(queries, inv_in, inv_out, store)
    return chunks, mine


def visit_raw_kernel(count, *refs):
    pieces = refs[:count]
    in_ref, out_ref, slab_ref, scores_ref, turned, left, held = refs[count:]
    _, groups, rows, _ = scores_ref.shape
    at = 0
    for piece in pieces:
        n = piece.shape[0] * piece.shape[1]
        held[at : at + n] = piece[...].reshape(n, piece.shape[2])
        at += n
    blocks = precondition(held[...], in_ref[0], out_ref[0], turned, left)
    for index, block in enumerate(blocks):
        held[:, index * WIDE : (index + 1) * WIDE] = block
    add_scores(held[...], slab_ref[...], scores_ref)


def visit_raw(raw, inv_in, inv_out, store):
    modules, side, _ = inv_in.shape
    size = side * side
    examples = store.shape[0]
    pieces = [upper for upper, _ in raw] + [lower for _, lower in raw]
    groups = pieces[0].shape[0]
    counts = [upper.shape[1] for upper, _ in raw]
    n = 2 * groups * sum(counts)
    small = pl.BlockSpec((1, side, side), lambda m: (m, 0, 0))
    scores = pl.pallas_call(
        functools.partial(visit_raw_kernel, len(pieces)),
        grid=(modules,),
        in_specs=[pl.BlockSpec((*p.shape[:2], size), lambda m: (0, 0, m)) for p in pieces]
        + [small, small, pl.BlockSpec((examples, size), lambda m: (0, m))],
        out_specs=pl.BlockSpec((2, groups, sum(counts), examples), lambda m: (0, 0, 0, 0)),
        out_shape=jax.ShapeDtypeStruct((2, groups, sum(counts), examples), jnp.float32),
        scratch_shapes=[
            pltpu.VMEM((side, side // LOW, LOW, n), jnp.float32),
            pltpu.VMEM((side, side // LOW, LOW, n), jnp.float32),
            pltpu.VMEM((n, size), jnp.bfloat16),
        ],
        compiler_params=pltpu.CompilerParams(vmem_limit_bytes=VMEM),
        name="visit_raw",
    )(*pieces, inv_in, inv_out, store)
    flat = scores.reshape(2, -1, examples)
    at, found = 0, []
    for count in counts:
        found.append(flat[:, at : at + groups * count].reshape(2, groups, count, examples))
        at += groups * count
    return jnp.concatenate(found, axis=2)


def visit_kernel(upper_ref, lower_ref, slab_ref, scores_ref):
    groups, rows, width = upper_ref.shape
    both = jnp.concatenate(
        [upper_ref[...].reshape(groups * rows, width), lower_ref[...].reshape(groups * rows, width)]
    )
    add_scores(both, slab_ref[...], scores_ref)


def visit(upper, lower, store, first, unit):
    groups, rows, width = upper.shape
    examples = store.shape[0]
    block = pl.BlockSpec((groups, rows, unit), lambda s: (0, 0, s))
    return pl.pallas_call(
        visit_kernel,
        grid=(width // unit,),
        in_specs=[block, block, pl.BlockSpec((examples, unit), lambda s: (0, s + first))],
        out_specs=pl.BlockSpec((2, groups, rows, examples), lambda s: (0, 0, 0, 0)),
        out_shape=jax.ShapeDtypeStruct((2, groups, rows, examples), jnp.float32),
        compiler_params=pltpu.CompilerParams(vmem_limit_bytes=VMEM),
        name="visit",
    )(upper, lower, store)


def shifted(value, axis, steps):
    count = lax.axis_size(axis)
    pairs = [(source, (source + steps) % count) for source in range(count)]
    return lax.ppermute(value, axis, pairs)


def grp_sum(part, dim):
    groups = lax.axis_size("grp")
    me = lax.axis_index("grp")
    total = lax.dynamic_index_in_dim(part, me, dim, keepdims=False)
    for turn in range(1, groups):
        share = lax.dynamic_index_in_dim(part, (me + turn) % groups, dim, keepdims=False)
        total = total + shifted(share, "grp", turn)
    return total


def to_owner(part, steps):
    ex = lax.axis_size("ex")
    groups = lax.axis_size("grp")
    me = lax.axis_index("grp")
    total = None
    for turn in range(groups):
        share = lax.dynamic_index_in_dim(part, (me + turn) % groups, 0, keepdims=False)
        pairs = [
            (b * groups + g, ((b + steps) % ex) * groups + (g + turn) % groups)
            for b in range(ex)
            for g in range(groups)
        ]
        arrived = lax.ppermute(share, ("ex", "grp"), pairs)
        total = arrived if total is None else total + arrived
    return total


def body(queries, inv_in, inv_out, store, listed):
    groups = lax.axis_size("grp")
    rows = queries.shape[0] // groups
    dims = queries.shape[1]
    unit = dims // sum(PIECES)
    bounds = [0]
    for part in CHUNKS:
        bounds.append(bounds[-1] + rows * part // sum(CHUNKS))
    together = lax.optimization_barrier

    def send(value):
        return shifted(value, "ex", -1), shifted(value, "ex", 1)

    split = queries.reshape(groups, rows, dims)
    first = lax.optimization_barrier(split[:, : bounds[1]])
    raw_one = send(first)
    raw_two = send(split[:, bounds[1] : bounds[2]])
    queries, raw_one = together((queries, raw_one))
    (a, b, c), mine = own(queries, inv_in, inv_out, store, groups, bounds[2:])
    cuts = []
    start = 0
    for count in PIECES:
        cuts.append(c[..., start * unit : (start + count) * unit])
        start += count

    came_a = send(a)
    b, raw_two = together((b, raw_two))
    came_b = send(b)
    scores_raw = visit_raw([raw_one, raw_two], inv_in, inv_out, store)
    cut, came_a, scores_raw = together((cuts[0], came_a, scores_raw))
    came_c = [send(cut)]
    scores_a = visit(*came_a, store, 0, unit)
    cut, came_b, scores_a = together((cuts[1], came_b, scores_a))
    came_c.append(send(cut))
    scores_b = visit(*came_b, store, 0, unit)
    cut, came_c[0], scores_b = together((cuts[2], came_c[0], scores_b))
    came_c.append(send(cut))
    both = grp_sum(jnp.concatenate([scores_raw, scores_a, scores_b], axis=2), 1)
    part = visit(*came_c[0], store, 0, unit)
    both, came_c[1] = together((both, came_c[1]))
    upper_scores = [shifted(both[0], "ex", 1)]
    lower_scores = [shifted(both[1], "ex", -1)]
    part = part + visit(*came_c[1], store, PIECES[0], unit)
    own_scores = grp_sum(mine, 0)
    part = part + visit(*came_c[2], store, PIECES[0] + PIECES[1], unit)
    upper_scores.append(to_owner(part[0], 1))
    lower_scores.append(to_owner(part[1], -1))

    scores = jnp.stack(
        [jnp.concatenate(upper_scores), own_scores, jnp.concatenate(lower_scores)]
    )
    return scores * mask(listed, rows, scores.shape[2])


def mask(listed, rows, examples):
    blocks = examples // SUB
    full = jnp.repeat(listed.astype(jnp.float32), QB, axis=0)
    start = lax.axis_index("grp") * rows
    mine = lax.dynamic_slice_in_dim(full, start, rows, 0)
    mine = mine.reshape(rows, 3, blocks).transpose(1, 0, 2)
    return jnp.repeat(mine, SUB, axis=2)


def solution(mesh):
    in_specs = (
        P("ex", "grp"),
        P("grp", None, None),
        P("grp", None, None),
        P("ex", "grp"),
        P("ex", None),
    )
    out_specs = P(None, ("ex", "grp"), None)
    return jax.shard_map(body, mesh=mesh, in_specs=in_specs, out_specs=out_specs, check_vma=False)
```

```python
import functools

import jax
import jax.numpy as jnp
from jax import lax
from jax.experimental import pallas as pl
from jax.experimental.pallas import tpu as pltpu
from jax.sharding import PartitionSpec as P

QB = 32
SUB = 64
CHUNKS = (2, 10, 4)
PIECES = (4, 2, 2)
WIDE = 256
LOW = 8
LANES = 128
VMEM = 56 * 1024 * 1024
NT = (((1,), (1,)), ((), ()))
TN = (((0,), (0,)), ((), ()))


def spread(matrix, rows_of, columns_of, keep):
    tall = jnp.dot(rows_of, matrix, preferred_element_type=jnp.float32)
    full = lax.dot_general(
        tall.astype(jnp.bfloat16), columns_of, NT, preferred_element_type=jnp.float32
    )
    return jnp.where(keep, full, 0.0).astype(jnp.bfloat16)


def precondition(x, inv_in, inv_out, turned, left):
    n, size = x.shape
    side = inv_in.shape[0]
    high = side // LOW
    per = WIDE // side

    def iota(shape, dim):
        return lax.broadcasted_iota(jnp.int32, shape, dim)

    def unit(rows, columns, test):
        hit = test(iota((rows, columns), 0), iota((rows, columns), 1))
        return jnp.where(hit, 1.0, 0.0).astype(jnp.bfloat16)

    identity = unit(WIDE, WIDE, lambda r, c: r == c)
    for block in range(size // WIDE):
        part = lax.dot_general(
            identity,
            x[:, block * WIDE : (block + 1) * WIDE],
            NT,
            preferred_element_type=jnp.float32,
        )
        turned[block * per : (block + 1) * per] = part.reshape(per, high, LOW, n)

    span = side * LOW
    expand = unit(span, side, lambda r, c: r // LOW == c)
    square = (span, span)
    factor = spread(inv_in, expand, expand, iota(square, 0) % LOW == iota(square, 1) % LOW)
    for part in range(high):
        piece = turned[:, part].reshape(span, n).astype(jnp.bfloat16)
        result = jnp.dot(factor, piece, preferred_element_type=jnp.float32)
        left[:, part] = result.astype(jnp.bfloat16).astype(jnp.float32).reshape(side, LOW, n)

    repeat = unit(WIDE, side, lambda r, c: r % side == c)
    square = (WIDE, WIDE)
    factor = spread(inv_out, repeat, repeat, iota(square, 0) // side == iota(square, 1) // side)
    blocks = []
    for block in range(size // WIDE):
        piece = left[block * per : (block + 1) * per].reshape(WIDE, n).astype(jnp.bfloat16)
        result = lax.dot_general(piece, factor, TN, preferred_element_type=jnp.float32)
        blocks.append(result.astype(jnp.bfloat16))
    return blocks


def add_scores(rows, slab, out_ref):
    part = lax.dot_general(rows, slab, NT, preferred_element_type=jnp.float32)

    @pl.when(pl.program_id(0) == 0)
    def _():
        out_ref[...] = part.reshape(out_ref.shape)

    @pl.when(pl.program_id(0) != 0)
    def _():
        out_ref[...] += part.reshape(out_ref.shape)


def own_kernel(bounds, x_ref, in_ref, out_ref, slab_ref, *rest):
    chunks, scores_ref, (turned, left, held) = rest[:-4], rest[-4], rest[-3:]
    n = x_ref.shape[0]
    groups = scores_ref.shape[0]
    rows = n // groups
    blocks = precondition(x_ref[...], in_ref[0], out_ref[0], turned, left)
    for index, block in enumerate(blocks):
        cut = pl.ds(index * WIDE, WIDE)
        held[:, cut] = block
        for chunk, low, top in zip(chunks, bounds[:-1], bounds[1:]):
            for group in range(groups):
                chunk[group, :, cut] = block[group * rows + low : group * rows + top]
    add_scores(held[...], slab_ref[...], scores_ref)


def own(queries, inv_in, inv_out, store, groups, bounds):
    n, dims = queries.shape
    modules, side, _ = inv_in.shape
    size = side * side
    examples = store.shape[0]
    small = pl.BlockSpec((1, side, side), lambda m: (m, 0, 0))
    sizes = [top - low for low, top in zip(bounds[:-1], bounds[1:])]
    *chunks, mine = pl.pallas_call(
        functools.partial(own_kernel, bounds),
        grid=(modules,),
        in_specs=[
            pl.BlockSpec((n, size), lambda m: (0, m)),
            small,
            small,
            pl.BlockSpec((examples, size), lambda m: (0, m)),
        ],
        out_specs=[pl.BlockSpec((groups, c, size), lambda m: (0, 0, m)) for c in sizes]
        + [pl.BlockSpec((groups, n // groups, examples), lambda m: (0, 0, 0))],
        out_shape=[jax.ShapeDtypeStruct((groups, c, dims), jnp.bfloat16) for c in sizes]
        + [jax.ShapeDtypeStruct((groups, n // groups, examples), jnp.float32)],
        scratch_shapes=[
            pltpu.VMEM((side, side // LOW, LOW, n), jnp.float32),
            pltpu.VMEM((side, side // LOW, LOW, n), jnp.float32),
            pltpu.VMEM((n, size), jnp.bfloat16),
        ],
        compiler_params=pltpu.CompilerParams(vmem_limit_bytes=VMEM),
        name="own",
    )(queries, inv_in, inv_out, store)
    return chunks, mine


def visit_raw_kernel(count, *refs):
    pieces = refs[:count]
    in_ref, out_ref, slab_ref, _, scores_ref, turned, left, held = refs[count:]
    _, groups, rows, _ = scores_ref.shape
    at = 0
    for piece in pieces:
        n = piece.shape[0] * piece.shape[1]
        held[at : at + n] = piece[...].reshape(n, piece.shape[2])
        at += n
    blocks = precondition(held[...], in_ref[0], out_ref[0], turned, left)
    for index, block in enumerate(blocks):
        held[:, index * WIDE : (index + 1) * WIDE] = block
    add_scores(held[...], slab_ref[...], scores_ref)


def visit_raw(raw, inv_in, inv_out, store, word):
    modules, side, _ = inv_in.shape
    size = side * side
    examples = store.shape[0]
    pieces = [upper for upper, _ in raw] + [lower for _, lower in raw]
    groups = pieces[0].shape[0]
    counts = [upper.shape[1] for upper, _ in raw]
    n = 2 * groups * sum(counts)
    small = pl.BlockSpec((1, side, side), lambda m: (m, 0, 0))
    scores = pl.pallas_call(
        functools.partial(visit_raw_kernel, len(pieces)),
        grid=(modules,),
        in_specs=[pl.BlockSpec((*p.shape[:2], size), lambda m: (0, 0, m)) for p in pieces]
        + [small, small, pl.BlockSpec((examples, size), lambda m: (0, m))]
        + [pl.BlockSpec(memory_space=pl.ANY)],
        out_specs=pl.BlockSpec((2, groups, sum(counts), examples), lambda m: (0, 0, 0, 0)),
        out_shape=jax.ShapeDtypeStruct((2, groups, sum(counts), examples), jnp.float32),
        scratch_shapes=[
            pltpu.VMEM((side, side // LOW, LOW, n), jnp.float32),
            pltpu.VMEM((side, side // LOW, LOW, n), jnp.float32),
            pltpu.VMEM((n, size), jnp.bfloat16),
        ],
        compiler_params=pltpu.CompilerParams(vmem_limit_bytes=VMEM),
        name="visit_raw",
    )(*pieces, inv_in, inv_out, store, word)
    flat = scores.reshape(2, -1, examples)
    at, found = 0, []
    for count in counts:
        found.append(flat[:, at : at + groups * count].reshape(2, groups, count, examples))
        at += groups * count
    return jnp.concatenate(found, axis=2)


def visit_kernel(upper_ref, lower_ref, slab_ref, _, scores_ref):
    groups, rows, width = upper_ref.shape
    both = jnp.concatenate(
        [upper_ref[...].reshape(groups * rows, width), lower_ref[...].reshape(groups * rows, width)]
    )
    add_scores(both, slab_ref[...], scores_ref)


def visit(upper, lower, store, first, unit, word):
    groups, rows, width = upper.shape
    examples = store.shape[0]
    block = pl.BlockSpec((groups, rows, unit), lambda s: (0, 0, s))
    return pl.pallas_call(
        visit_kernel,
        grid=(width // unit,),
        in_specs=[
            block,
            block,
            pl.BlockSpec((examples, unit), lambda s: (0, s + first)),
            pl.BlockSpec(memory_space=pl.ANY),
        ],
        out_specs=pl.BlockSpec((2, groups, rows, examples), lambda s: (0, 0, 0, 0)),
        out_shape=jax.ShapeDtypeStruct((2, groups, rows, examples), jnp.float32),
        compiler_params=pltpu.CompilerParams(vmem_limit_bytes=VMEM),
        name="visit",
    )(upper, lower, store, word)


def shifted(value, axis, steps):
    count = lax.axis_size(axis)
    pairs = [(source, (source + steps) % count) for source in range(count)]
    return lax.ppermute(value, axis, pairs)


def grp_sum(part, dim):
    groups = lax.axis_size("grp")
    me = lax.axis_index("grp")
    total = lax.dynamic_index_in_dim(part, me, dim, keepdims=False)
    for turn in range(1, groups):
        share = lax.dynamic_index_in_dim(part, (me + turn) % groups, dim, keepdims=False)
        total = total + shifted(share, "grp", turn)
    return total


def to_owner(part, steps):
    ex = lax.axis_size("ex")
    groups = lax.axis_size("grp")
    me = lax.axis_index("grp")
    total = None
    for turn in range(groups):
        share = lax.dynamic_index_in_dim(part, (me + turn) % groups, 0, keepdims=False)
        pairs = [
            (b * groups + g, ((b + steps) % ex) * groups + (g + turn) % groups)
            for b in range(ex)
            for g in range(groups)
        ]
        arrived = lax.ppermute(share, ("ex", "grp"), pairs)
        total = arrived if total is None else total + arrived
    return total


def body(queries, inv_in, inv_out, store, listed):
    groups = lax.axis_size("grp")
    rows = queries.shape[0] // groups
    dims = queries.shape[1]
    unit = dims // sum(PIECES)
    bounds = [0]
    for part in CHUNKS:
        bounds.append(bounds[-1] + rows * part // sum(CHUNKS))
    together = lax.optimization_barrier

    def send(value):
        return shifted(value, "ex", -1), shifted(value, "ex", 1)

    split = queries.reshape(groups, rows, dims)
    first, queries = together((split[:, : bounds[1]], queries))
    came_raw = send(first)
    (a, c), mine = own(queries, inv_in, inv_out, store, groups, bounds[1:])
    cuts = []
    start = 0
    for count in PIECES:
        cuts.append(c[..., start * unit : (start + count) * unit])
        start += count

    def both_there(came, work):
        word, came, work = together((came[0][0, :, :LANES], came, work))
        pairs = [(i, i ^ 1) for i in range(lax.axis_size("ex"))]
        return lax.ppermute(word, "ex", pairs), came, work

    word, came_raw, mine = both_there(came_raw, mine)
    a, cut, word = together((a, cuts[0], word))
    came_a = send(a)
    came_c = [send(cut)]
    scores_raw = visit_raw([came_raw], inv_in, inv_out, store, word)
    own_scores = grp_sum(mine, 0)
    word, came_a, (scores_raw, own_scores) = both_there(came_a, (scores_raw, own_scores))
    cut, word = together((cuts[1], word))
    came_c.append(send(cut))
    scores_a = visit(*came_a, store, 0, unit, word)
    both = grp_sum(jnp.concatenate([scores_raw, scores_a], axis=2), 1)
    word, came_c[0], both = both_there(came_c[0], both)
    cut, word = together((cuts[2], word))
    came_c.append(send(cut))
    part = visit(*came_c[0], store, 0, unit, word)
    both, came_c[1] = together((both, came_c[1]))
    upper_scores = [shifted(both[0], "ex", 1)]
    lower_scores = [shifted(both[1], "ex", -1)]
    part = part + visit(*came_c[1], store, PIECES[0], unit, word)
    part = part + visit(*came_c[2], store, PIECES[0] + PIECES[1], unit, word)
    upper_scores.append(to_owner(part[0], 1))
    lower_scores.append(to_owner(part[1], -1))

    scores = jnp.stack(
        [jnp.concatenate(upper_scores), own_scores, jnp.concatenate(lower_scores)]
    )
    return scores * mask(listed, rows, scores.shape[2])


def mask(listed, rows, examples):
    blocks = examples // SUB
    full = jnp.repeat(listed.astype(jnp.float32), QB, axis=0)
    start = lax.axis_index("grp") * rows
    mine = lax.dynamic_slice_in_dim(full, start, rows, 0)
    mine = mine.reshape(rows, 3, blocks).transpose(1, 0, 2)
    return jnp.repeat(mine, SUB, axis=2)


def solution(mesh):
    in_specs = (
        P("ex", "grp"),
        P("grp", None, None),
        P("grp", None, None),
        P("ex", "grp"),
        P("ex", None),
    )
    out_specs = P(None, ("ex", "grp"), None)
    return jax.shard_map(body, mesh=mesh, in_specs=in_specs, out_specs=out_specs, check_vma=False)
```

```python
import functools

import jax
import jax.numpy as jnp
from jax import lax
from jax.experimental import pallas as pl
from jax.experimental.pallas import tpu as pltpu
from jax.sharding import PartitionSpec as P

QB = 32
SUB = 64
CHUNKS = (2, 10, 4)
PIECES = (4, 3, 1)
WIDE = 256
LOW = 8
LANES = 128
VMEM = 56 * 1024 * 1024
NT = (((1,), (1,)), ((), ()))
TN = (((0,), (0,)), ((), ()))


def spread(matrix, rows_of, columns_of, keep):
    tall = jnp.dot(rows_of, matrix, preferred_element_type=jnp.float32)
    full = lax.dot_general(
        tall.astype(jnp.bfloat16), columns_of, NT, preferred_element_type=jnp.float32
    )
    return jnp.where(keep, full, 0.0).astype(jnp.bfloat16)


def precondition(x, inv_in, inv_out, turned, left):
    n, size = x.shape
    side = inv_in.shape[0]
    high = side // LOW
    per = WIDE // side

    def iota(shape, dim):
        return lax.broadcasted_iota(jnp.int32, shape, dim)

    def unit(rows, columns, test):
        hit = test(iota((rows, columns), 0), iota((rows, columns), 1))
        return jnp.where(hit, 1.0, 0.0).astype(jnp.bfloat16)

    identity = unit(WIDE, WIDE, lambda r, c: r == c)
    for block in range(size // WIDE):
        part = lax.dot_general(
            identity,
            x[:, block * WIDE : (block + 1) * WIDE],
            NT,
            preferred_element_type=jnp.float32,
        )
        turned[block * per : (block + 1) * per] = part.reshape(per, high, LOW, n)

    span = side * LOW
    expand = unit(span, side, lambda r, c: r // LOW == c)
    square = (span, span)
    factor = spread(inv_in, expand, expand, iota(square, 0) % LOW == iota(square, 1) % LOW)
    for part in range(high):
        piece = turned[:, part].reshape(span, n).astype(jnp.bfloat16)
        result = jnp.dot(factor, piece, preferred_element_type=jnp.float32)
        left[:, part] = result.astype(jnp.bfloat16).astype(jnp.float32).reshape(side, LOW, n)

    repeat = unit(WIDE, side, lambda r, c: r % side == c)
    square = (WIDE, WIDE)
    factor = spread(inv_out, repeat, repeat, iota(square, 0) // side == iota(square, 1) // side)
    blocks = []
    for block in range(size // WIDE):
        piece = left[block * per : (block + 1) * per].reshape(WIDE, n).astype(jnp.bfloat16)
        result = lax.dot_general(piece, factor, TN, preferred_element_type=jnp.float32)
        blocks.append(result.astype(jnp.bfloat16))
    return blocks


def add_scores(rows, slab, out_ref, base=None):
    part = lax.dot_general(rows, slab, NT, preferred_element_type=jnp.float32)

    @pl.when(pl.program_id(0) == 0)
    def _():
        first = part.reshape(out_ref.shape)
        out_ref[...] = first if base is None else base[...] + first

    @pl.when(pl.program_id(0) != 0)
    def _():
        out_ref[...] += part.reshape(out_ref.shape)


def own_kernel(bounds, x_ref, in_ref, out_ref, slab_ref, *rest):
    chunks, scores_ref, (turned, left, held) = rest[:-4], rest[-4], rest[-3:]
    n = x_ref.shape[0]
    groups = scores_ref.shape[0]
    rows = n // groups
    blocks = precondition(x_ref[...], in_ref[0], out_ref[0], turned, left)
    for index, block in enumerate(blocks):
        cut = pl.ds(index * WIDE, WIDE)
        held[:, cut] = block
        for chunk, low, top in zip(chunks, bounds[:-1], bounds[1:]):
            for group in range(groups):
                chunk[group, :, cut] = block[group * rows + low : group * rows + top]
    add_scores(held[...], slab_ref[...], scores_ref)


def own(queries, inv_in, inv_out, store, groups, bounds):
    n, dims = queries.shape
    modules, side, _ = inv_in.shape
    size = side * side
    examples = store.shape[0]
    small = pl.BlockSpec((1, side, side), lambda m: (m, 0, 0))
    sizes = [top - low for low, top in zip(bounds[:-1], bounds[1:])]
    *chunks, mine = pl.pallas_call(
        functools.partial(own_kernel, bounds),
        grid=(modules,),
        in_specs=[
            pl.BlockSpec((n, size), lambda m: (0, m)),
            small,
            small,
            pl.BlockSpec((examples, size), lambda m: (0, m)),
        ],
        out_specs=[pl.BlockSpec((groups, c, size), lambda m: (0, 0, m)) for c in sizes]
        + [pl.BlockSpec((groups, n // groups, examples), lambda m: (0, 0, 0))],
        out_shape=[jax.ShapeDtypeStruct((groups, c, dims), jnp.bfloat16) for c in sizes]
        + [jax.ShapeDtypeStruct((groups, n // groups, examples), jnp.float32)],
        scratch_shapes=[
            pltpu.VMEM((side, side // LOW, LOW, n), jnp.float32),
            pltpu.VMEM((side, side // LOW, LOW, n), jnp.float32),
            pltpu.VMEM((n, size), jnp.bfloat16),
        ],
        compiler_params=pltpu.CompilerParams(vmem_limit_bytes=VMEM),
        name="own",
    )(queries, inv_in, inv_out, store)
    return chunks, mine


def visit_raw_kernel(count, *refs):
    pieces = refs[:count]
    in_ref, out_ref, slab_ref, _, scores_ref, turned, left, held = refs[count:]
    _, groups, rows, _ = scores_ref.shape
    at = 0
    for piece in pieces:
        n = piece.shape[0] * piece.shape[1]
        held[at : at + n] = piece[...].reshape(n, piece.shape[2])
        at += n
    blocks = precondition(held[...], in_ref[0], out_ref[0], turned, left)
    for index, block in enumerate(blocks):
        held[:, index * WIDE : (index + 1) * WIDE] = block
    add_scores(held[...], slab_ref[...], scores_ref)


def visit_raw(raw, inv_in, inv_out, store, word):
    modules, side, _ = inv_in.shape
    size = side * side
    examples = store.shape[0]
    pieces = [upper for upper, _ in raw] + [lower for _, lower in raw]
    groups = pieces[0].shape[0]
    counts = [upper.shape[1] for upper, _ in raw]
    n = 2 * groups * sum(counts)
    small = pl.BlockSpec((1, side, side), lambda m: (m, 0, 0))
    scores = pl.pallas_call(
        functools.partial(visit_raw_kernel, len(pieces)),
        grid=(modules,),
        in_specs=[pl.BlockSpec((*p.shape[:2], size), lambda m: (0, 0, m)) for p in pieces]
        + [small, small, pl.BlockSpec((examples, size), lambda m: (0, m))]
        + [pl.BlockSpec(memory_space=pl.ANY)],
        out_specs=pl.BlockSpec((2, groups, sum(counts), examples), lambda m: (0, 0, 0, 0)),
        out_shape=jax.ShapeDtypeStruct((2, groups, sum(counts), examples), jnp.float32),
        scratch_shapes=[
            pltpu.VMEM((side, side // LOW, LOW, n), jnp.float32),
            pltpu.VMEM((side, side // LOW, LOW, n), jnp.float32),
            pltpu.VMEM((n, size), jnp.bfloat16),
        ],
        compiler_params=pltpu.CompilerParams(vmem_limit_bytes=VMEM),
        name="visit_raw",
    )(*pieces, inv_in, inv_out, store, word)
    flat = scores.reshape(2, -1, examples)
    at, found = 0, []
    for count in counts:
        found.append(flat[:, at : at + groups * count].reshape(2, groups, count, examples))
        at += groups * count
    return jnp.concatenate(found, axis=2)


def visit_kernel(count, upper_ref, lower_ref, slab_ref, *rest):
    *base, scores_ref = rest[count:]
    groups, rows, width = upper_ref.shape
    both = jnp.concatenate(
        [upper_ref[...].reshape(groups * rows, width), lower_ref[...].reshape(groups * rows, width)]
    )
    add_scores(both, slab_ref[...], scores_ref, *base)


def visit(upper, lower, store, first, unit, words, *base):
    groups, rows, width = upper.shape
    examples = store.shape[0]
    block = pl.BlockSpec((groups, rows, unit), lambda s: (0, 0, s))
    whole = pl.BlockSpec((2, groups, rows, examples), lambda s: (0, 0, 0, 0))
    return pl.pallas_call(
        functools.partial(visit_kernel, len(words)),
        grid=(width // unit,),
        in_specs=[
            block,
            block,
            pl.BlockSpec((examples, unit), lambda s: (0, s + first)),
        ]
        + [pl.BlockSpec(memory_space=pl.ANY) for _ in words]
        + [whole for _ in base],
        out_specs=whole,
        out_shape=jax.ShapeDtypeStruct((2, groups, rows, examples), jnp.float32),
        compiler_params=pltpu.CompilerParams(vmem_limit_bytes=VMEM),
        name="visit",
    )(upper, lower, store, *words, *base)


def shifted(value, axis, steps):
    count = lax.axis_size(axis)
    pairs = [(source, (source + steps) % count) for source in range(count)]
    return lax.ppermute(value, axis, pairs)


def grp_sum(part, dim):
    groups = lax.axis_size("grp")
    me = lax.axis_index("grp")
    total = lax.dynamic_index_in_dim(part, me, dim, keepdims=False)
    for turn in range(1, groups):
        share = lax.dynamic_index_in_dim(part, (me + turn) % groups, dim, keepdims=False)
        total = total + shifted(share, "grp", turn)
    return total


def to_owner(part, steps):
    ex = lax.axis_size("ex")
    groups = lax.axis_size("grp")
    me = lax.axis_index("grp")
    total = None
    for turn in range(groups):
        share = lax.dynamic_index_in_dim(part, (me + turn) % groups, 0, keepdims=False)
        pairs = [
            (b * groups + g, ((b + steps) % ex) * groups + (g + turn) % groups)
            for b in range(ex)
            for g in range(groups)
        ]
        arrived = lax.ppermute(share, ("ex", "grp"), pairs)
        total = arrived if total is None else total + arrived
    return total


def body(queries, inv_in, inv_out, store, listed):
    groups = lax.axis_size("grp")
    rows = queries.shape[0] // groups
    dims = queries.shape[1]
    unit = dims // sum(PIECES)
    bounds = [0]
    for part in CHUNKS:
        bounds.append(bounds[-1] + rows * part // sum(CHUNKS))
    together = lax.optimization_barrier

    def send(value):
        return shifted(value, "ex", -1), shifted(value, "ex", 1)

    split = queries.reshape(groups, rows, dims)
    first, queries = together((split[:, : bounds[1]], queries))
    came_raw = send(first)
    (a, c), mine = own(queries, inv_in, inv_out, store, groups, bounds[1:])
    cuts = []
    start = 0
    for count in PIECES:
        cuts.append(c[..., start * unit : (start + count) * unit])
        start += count

    def both_there(came, work):
        word, came, work = together((came[0][0, :, :LANES], came, work))
        pairs = [(i, i ^ 1) for i in range(lax.axis_size("ex"))]
        return lax.ppermute(word, "ex", pairs), came, work

    word, came_raw, (mine, cuts) = both_there(came_raw, (mine, cuts))
    a, cut, word = together((a, cuts[0], word))
    came_a = send(a)
    came_c = [send(cut)]
    scores_raw = visit_raw([came_raw], inv_in, inv_out, store, word)
    own_scores = grp_sum(mine, 0)
    word, came_a, (scores_raw, own_scores) = both_there(came_a, (scores_raw, own_scores))
    cut, word = together((cuts[1], word))
    came_c.append(send(cut))
    scores_a = visit(*came_a, store, 0, unit, [word])
    both = grp_sum(jnp.concatenate([scores_raw, scores_a], axis=2), 1)
    word, came_c[0], both = both_there(came_c[0], both)
    cut, word = together((cuts[2], word))
    came_c.append(send(cut))
    part = visit(*came_c[0], store, 0, unit, [word])
    both, came_c[1], part = together((both, came_c[1], part))
    returned = shifted(both[0], "ex", 1), shifted(both[1], "ex", -1)
    part = visit(*came_c[1], store, PIECES[0], unit, [word], part)
    part = visit(*came_c[2], store, PIECES[0] + PIECES[1], unit, returned, part)
    upper_scores = [returned[0], to_owner(part[0], 1)]
    lower_scores = [returned[1], to_owner(part[1], -1)]

    scores = jnp.stack(
        [jnp.concatenate(upper_scores), own_scores, jnp.concatenate(lower_scores)]
    )
    return scores * mask(listed, rows, scores.shape[2])


def mask(listed, rows, examples):
    blocks = examples // SUB
    full = jnp.repeat(listed.astype(jnp.float32), QB, axis=0)
    start = lax.axis_index("grp") * rows
    mine = lax.dynamic_slice_in_dim(full, start, rows, 0)
    mine = mine.reshape(rows, 3, blocks).transpose(1, 0, 2)
    return jnp.repeat(mine, SUB, axis=2)


def solution(mesh):
    in_specs = (
        P("ex", "grp"),
        P("grp", None, None),
        P("grp", None, None),
        P("ex", "grp"),
        P("ex", None),
    )
    out_specs = P(None, ("ex", "grp"), None)
    return jax.shard_map(body, mesh=mesh, in_specs=in_specs, out_specs=out_specs, check_vma=False)
```

```python
import functools

import jax
import jax.numpy as jnp
from jax import lax
from jax.experimental import pallas as pl
from jax.experimental.pallas import tpu as pltpu
from jax.sharding import PartitionSpec as P

QB = 32
SUB = 64
CHUNKS = (2, 8, 6)
PIECES = (5, 2, 1)
WIDE = 256
LOW = 8
LANES = 128
VMEM = 56 * 1024 * 1024
NT = (((1,), (1,)), ((), ()))
TN = (((0,), (0,)), ((), ()))


def spread(matrix, rows_of, columns_of, keep):
    tall = jnp.dot(rows_of, matrix, preferred_element_type=jnp.float32)
    full = lax.dot_general(
        tall.astype(jnp.bfloat16), columns_of, NT, preferred_element_type=jnp.float32
    )
    return jnp.where(keep, full, 0.0).astype(jnp.bfloat16)


def precondition(x, inv_in, inv_out, turned, left):
    n, size = x.shape
    side = inv_in.shape[0]
    high = side // LOW
    per = WIDE // side

    def iota(shape, dim):
        return lax.broadcasted_iota(jnp.int32, shape, dim)

    def unit(rows, columns, test):
        hit = test(iota((rows, columns), 0), iota((rows, columns), 1))
        return jnp.where(hit, 1.0, 0.0).astype(jnp.bfloat16)

    identity = unit(WIDE, WIDE, lambda r, c: r == c)
    for block in range(size // WIDE):
        part = lax.dot_general(
            identity,
            x[:, block * WIDE : (block + 1) * WIDE],
            NT,
            preferred_element_type=jnp.float32,
        )
        turned[block * per : (block + 1) * per] = part.reshape(per, high, LOW, n)

    span = side * LOW
    expand = unit(span, side, lambda r, c: r // LOW == c)
    square = (span, span)
    factor = spread(inv_in, expand, expand, iota(square, 0) % LOW == iota(square, 1) % LOW)
    for part in range(high):
        piece = turned[:, part].reshape(span, n).astype(jnp.bfloat16)
        result = jnp.dot(factor, piece, preferred_element_type=jnp.float32)
        left[:, part] = result.astype(jnp.bfloat16).astype(jnp.float32).reshape(side, LOW, n)

    repeat = unit(WIDE, side, lambda r, c: r % side == c)
    square = (WIDE, WIDE)
    factor = spread(inv_out, repeat, repeat, iota(square, 0) // side == iota(square, 1) // side)
    blocks = []
    for block in range(size // WIDE):
        piece = left[block * per : (block + 1) * per].reshape(WIDE, n).astype(jnp.bfloat16)
        result = lax.dot_general(piece, factor, TN, preferred_element_type=jnp.float32)
        blocks.append(result.astype(jnp.bfloat16))
    return blocks


def add_scores(rows, slab, out_ref, base=None):
    part = lax.dot_general(rows, slab, NT, preferred_element_type=jnp.float32)

    @pl.when(pl.program_id(0) == 0)
    def _():
        first = part.reshape(out_ref.shape)
        out_ref[...] = first if base is None else base[...] + first

    @pl.when(pl.program_id(0) != 0)
    def _():
        out_ref[...] += part.reshape(out_ref.shape)


def own_kernel(bounds, x_ref, in_ref, out_ref, slab_ref, *rest):
    chunks, scores_ref, (turned, left, held) = rest[:-4], rest[-4], rest[-3:]
    n = x_ref.shape[0]
    groups = scores_ref.shape[0]
    rows = n // groups
    blocks = precondition(x_ref[...], in_ref[0], out_ref[0], turned, left)
    for index, block in enumerate(blocks):
        cut = pl.ds(index * WIDE, WIDE)
        held[:, cut] = block
        for chunk, low, top in zip(chunks, bounds[:-1], bounds[1:]):
            for group in range(groups):
                chunk[group, :, cut] = block[group * rows + low : group * rows + top]
    add_scores(held[...], slab_ref[...], scores_ref)


def own(queries, inv_in, inv_out, store, groups, bounds):
    n, dims = queries.shape
    modules, side, _ = inv_in.shape
    size = side * side
    examples = store.shape[0]
    small = pl.BlockSpec((1, side, side), lambda m: (m, 0, 0))
    sizes = [top - low for low, top in zip(bounds[:-1], bounds[1:])]
    *chunks, mine = pl.pallas_call(
        functools.partial(own_kernel, bounds),
        grid=(modules,),
        in_specs=[
            pl.BlockSpec((n, size), lambda m: (0, m)),
            small,
            small,
            pl.BlockSpec((examples, size), lambda m: (0, m)),
        ],
        out_specs=[pl.BlockSpec((groups, c, size), lambda m: (0, 0, m)) for c in sizes]
        + [pl.BlockSpec((groups, n // groups, examples), lambda m: (0, 0, 0))],
        out_shape=[jax.ShapeDtypeStruct((groups, c, dims), jnp.bfloat16) for c in sizes]
        + [jax.ShapeDtypeStruct((groups, n // groups, examples), jnp.float32)],
        scratch_shapes=[
            pltpu.VMEM((side, side // LOW, LOW, n), jnp.float32),
            pltpu.VMEM((side, side // LOW, LOW, n), jnp.float32),
            pltpu.VMEM((n, size), jnp.bfloat16),
        ],
        compiler_params=pltpu.CompilerParams(vmem_limit_bytes=VMEM),
        name="own",
    )(queries, inv_in, inv_out, store)
    return chunks, mine


def visit_raw_kernel(count, *refs):
    pieces = refs[:count]
    in_ref, out_ref, slab_ref, _, scores_ref, turned, left, held = refs[count:]
    _, groups, rows, _ = scores_ref.shape
    at = 0
    for piece in pieces:
        n = piece.shape[0] * piece.shape[1]
        held[at : at + n] = piece[...].reshape(n, piece.shape[2])
        at += n
    blocks = precondition(held[...], in_ref[0], out_ref[0], turned, left)
    for index, block in enumerate(blocks):
        held[:, index * WIDE : (index + 1) * WIDE] = block
    add_scores(held[...], slab_ref[...], scores_ref)


def visit_raw(raw, inv_in, inv_out, store, word):
    modules, side, _ = inv_in.shape
    size = side * side
    examples = store.shape[0]
    pieces = [upper for upper, _ in raw] + [lower for _, lower in raw]
    groups = pieces[0].shape[0]
    counts = [upper.shape[1] for upper, _ in raw]
    n = 2 * groups * sum(counts)
    small = pl.BlockSpec((1, side, side), lambda m: (m, 0, 0))
    scores = pl.pallas_call(
        functools.partial(visit_raw_kernel, len(pieces)),
        grid=(modules,),
        in_specs=[pl.BlockSpec((*p.shape[:2], size), lambda m: (0, 0, m)) for p in pieces]
        + [small, small, pl.BlockSpec((examples, size), lambda m: (0, m))]
        + [pl.BlockSpec(memory_space=pl.ANY)],
        out_specs=pl.BlockSpec((2, groups, sum(counts), examples), lambda m: (0, 0, 0, 0)),
        out_shape=jax.ShapeDtypeStruct((2, groups, sum(counts), examples), jnp.float32),
        scratch_shapes=[
            pltpu.VMEM((side, side // LOW, LOW, n), jnp.float32),
            pltpu.VMEM((side, side // LOW, LOW, n), jnp.float32),
            pltpu.VMEM((n, size), jnp.bfloat16),
        ],
        compiler_params=pltpu.CompilerParams(vmem_limit_bytes=VMEM),
        name="visit_raw",
    )(*pieces, inv_in, inv_out, store, word)
    flat = scores.reshape(2, -1, examples)
    at, found = 0, []
    for count in counts:
        found.append(flat[:, at : at + groups * count].reshape(2, groups, count, examples))
        at += groups * count
    return jnp.concatenate(found, axis=2)


def visit_kernel(count, upper_ref, lower_ref, slab_ref, *rest):
    *base, scores_ref = rest[count:]
    groups, rows, width = upper_ref.shape
    both = jnp.concatenate(
        [upper_ref[...].reshape(groups * rows, width), lower_ref[...].reshape(groups * rows, width)]
    )
    add_scores(both, slab_ref[...], scores_ref, *base)


def visit(upper, lower, store, first, unit, words, *base):
    groups, rows, width = upper.shape
    examples = store.shape[0]
    block = pl.BlockSpec((groups, rows, unit), lambda s: (0, 0, s))
    whole = pl.BlockSpec((2, groups, rows, examples), lambda s: (0, 0, 0, 0))
    return pl.pallas_call(
        functools.partial(visit_kernel, len(words)),
        grid=(width // unit,),
        in_specs=[
            block,
            block,
            pl.BlockSpec((examples, unit), lambda s: (0, s + first)),
        ]
        + [pl.BlockSpec(memory_space=pl.ANY) for _ in words]
        + [whole for _ in base],
        out_specs=whole,
        out_shape=jax.ShapeDtypeStruct((2, groups, rows, examples), jnp.float32),
        compiler_params=pltpu.CompilerParams(vmem_limit_bytes=VMEM),
        name="visit",
    )(upper, lower, store, *words, *base)


def shifted(value, axis, steps):
    count = lax.axis_size(axis)
    pairs = [(source, (source + steps) % count) for source in range(count)]
    return lax.ppermute(value, axis, pairs)


def grp_sum(part, dim):
    groups = lax.axis_size("grp")
    me = lax.axis_index("grp")
    total = lax.dynamic_index_in_dim(part, me, dim, keepdims=False)
    for turn in range(1, groups):
        share = lax.dynamic_index_in_dim(part, (me + turn) % groups, dim, keepdims=False)
        total = total + shifted(share, "grp", turn)
    return total


def to_owner(part, steps):
    ex = lax.axis_size("ex")
    groups = lax.axis_size("grp")
    me = lax.axis_index("grp")
    total = None
    for turn in range(groups):
        share = lax.dynamic_index_in_dim(part, (me + turn) % groups, 0, keepdims=False)
        pairs = [
            (b * groups + g, ((b + steps) % ex) * groups + (g + turn) % groups)
            for b in range(ex)
            for g in range(groups)
        ]
        arrived = lax.ppermute(share, ("ex", "grp"), pairs)
        total = arrived if total is None else total + arrived
    return total


def body(queries, inv_in, inv_out, store, listed):
    groups = lax.axis_size("grp")
    rows = queries.shape[0] // groups
    dims = queries.shape[1]
    unit = dims // sum(PIECES)
    bounds = [0]
    for part in CHUNKS:
        bounds.append(bounds[-1] + rows * part // sum(CHUNKS))
    together = lax.optimization_barrier

    def send(value):
        return shifted(value, "ex", -1), shifted(value, "ex", 1)

    split = queries.reshape(groups, rows, dims)
    first, queries = together((split[:, : bounds[1]], queries))
    came_raw = send(first)
    (a, c), mine = own(queries, inv_in, inv_out, store, groups, bounds[1:])
    cuts = []
    start = 0
    for count in PIECES:
        cuts.append(c[..., start * unit : (start + count) * unit])
        start += count

    def both_there(came, work):
        word, came, work = together((came[0][0, :, :LANES], came, work))
        pairs = [(i, i ^ 1) for i in range(lax.axis_size("ex"))]
        return lax.ppermute(word, "ex", pairs), came, work

    word, came_raw, (mine, cuts) = both_there(came_raw, (mine, cuts))
    a, cut, word = together((a, cuts[0], word))
    came_a = send(a)
    came_c = [send(cut)]
    scores_raw = visit_raw([came_raw], inv_in, inv_out, store, word)
    own_scores = grp_sum(mine, 0)
    word, came_a, (scores_raw, own_scores) = both_there(came_a, (scores_raw, own_scores))
    cut, word = together((cuts[1], word))
    came_c.append(send(cut))
    scores_a = visit(*came_a, store, 0, unit, [word])
    both = grp_sum(jnp.concatenate([scores_raw, scores_a], axis=2), 1)
    word, came_c[0], both = both_there(came_c[0], both)
    cut, word = together((cuts[2], word))
    came_c.append(send(cut))
    part = visit(*came_c[0], store, 0, unit, [word])
    both, came_c[1], part = together((both, came_c[1], part))
    returned = shifted(both[0], "ex", 1), shifted(both[1], "ex", -1)
    part = visit(*came_c[1], store, PIECES[0], unit, [word], part)
    part = visit(*came_c[2], store, PIECES[0] + PIECES[1], unit, returned, part)
    upper_scores = [returned[0], to_owner(part[0], 1)]
    lower_scores = [returned[1], to_owner(part[1], -1)]

    scores = jnp.stack(
        [jnp.concatenate(upper_scores), own_scores, jnp.concatenate(lower_scores)]
    )
    return scores * mask(listed, rows, scores.shape[2])


def mask(listed, rows, examples):
    blocks = examples // SUB
    full = jnp.repeat(listed.astype(jnp.float32), QB, axis=0)
    start = lax.axis_index("grp") * rows
    mine = lax.dynamic_slice_in_dim(full, start, rows, 0)
    mine = mine.reshape(rows, 3, blocks).transpose(1, 0, 2)
    return jnp.repeat(mine, SUB, axis=2)


def solution(mesh):
    in_specs = (
        P("ex", "grp"),
        P("grp", None, None),
        P("grp", None, None),
        P("ex", "grp"),
        P("ex", None),
    )
    out_specs = P(None, ("ex", "grp"), None)
    return jax.shard_map(body, mesh=mesh, in_specs=in_specs, out_specs=out_specs, check_vma=False)
```

```python
import functools

import jax
import jax.numpy as jnp
from jax import lax
from jax.experimental import pallas as pl
from jax.experimental.pallas import tpu as pltpu
from jax.sharding import PartitionSpec as P

QB = 32
SUB = 64
CHUNKS = (2, 8, 6)
PIECES = (5, 2, 1)
WIDE = 256
LOW = 8
LANES = 128
VMEM = 56 * 1024 * 1024
NT = (((1,), (1,)), ((), ()))
TN = (((0,), (0,)), ((), ()))


def spread(matrix, rows_of, columns_of, keep):
    tall = jnp.dot(rows_of, matrix, preferred_element_type=jnp.float32)
    full = lax.dot_general(
        tall.astype(jnp.bfloat16), columns_of, NT, preferred_element_type=jnp.float32
    )
    return jnp.where(keep, full, 0.0).astype(jnp.bfloat16)


def precondition(x, inv_in, inv_out, turned, left):
    n, size = x.shape
    side = inv_in.shape[0]
    high = side // LOW
    per = WIDE // side

    def iota(shape, dim):
        return lax.broadcasted_iota(jnp.int32, shape, dim)

    def unit(rows, columns, test):
        hit = test(iota((rows, columns), 0), iota((rows, columns), 1))
        return jnp.where(hit, 1.0, 0.0).astype(jnp.bfloat16)

    identity = unit(WIDE, WIDE, lambda r, c: r == c)
    for block in range(size // WIDE):
        part = lax.dot_general(
            identity,
            x[:, block * WIDE : (block + 1) * WIDE],
            NT,
            preferred_element_type=jnp.float32,
        )
        turned[block * per : (block + 1) * per] = part.reshape(per, high, LOW, n)

    span = side * LOW
    expand = unit(span, side, lambda r, c: r // LOW == c)
    square = (span, span)
    factor = spread(inv_in, expand, expand, iota(square, 0) % LOW == iota(square, 1) % LOW)
    for part in range(high):
        piece = turned[:, part].reshape(span, n).astype(jnp.bfloat16)
        result = jnp.dot(factor, piece, preferred_element_type=jnp.float32)
        left[:, part] = result.astype(jnp.bfloat16).astype(jnp.float32).reshape(side, LOW, n)

    repeat = unit(WIDE, side, lambda r, c: r % side == c)
    square = (WIDE, WIDE)
    factor = spread(inv_out, repeat, repeat, iota(square, 0) // side == iota(square, 1) // side)
    blocks = []
    for block in range(size // WIDE):
        piece = left[block * per : (block + 1) * per].reshape(WIDE, n).astype(jnp.bfloat16)
        result = lax.dot_general(piece, factor, TN, preferred_element_type=jnp.float32)
        blocks.append(result.astype(jnp.bfloat16))
    return blocks


def add_scores(rows, slab, out_ref, base=None):
    part = lax.dot_general(rows, slab, NT, preferred_element_type=jnp.float32)

    @pl.when(pl.program_id(0) == 0)
    def _():
        first = part.reshape(out_ref.shape)
        out_ref[...] = first if base is None else base[...] + first

    @pl.when(pl.program_id(0) != 0)
    def _():
        out_ref[...] += part.reshape(out_ref.shape)


def own_kernel(bounds, x_ref, in_ref, out_ref, slab_ref, *rest):
    chunks, scores_ref, (turned, left, held) = rest[:-4], rest[-4], rest[-3:]
    n = x_ref.shape[0]
    groups = scores_ref.shape[0]
    rows = n // groups
    blocks = precondition(x_ref[...], in_ref[0], out_ref[0], turned, left)
    for index, block in enumerate(blocks):
        cut = pl.ds(index * WIDE, WIDE)
        held[:, cut] = block
        for chunk, low, top in zip(chunks, bounds[:-1], bounds[1:]):
            for group in range(groups):
                chunk[group, :, cut] = block[group * rows + low : group * rows + top]
    add_scores(held[...], slab_ref[...], scores_ref)


def own(queries, inv_in, inv_out, store, groups, bounds):
    n, dims = queries.shape
    modules, side, _ = inv_in.shape
    size = side * side
    examples = store.shape[0]
    small = pl.BlockSpec((1, side, side), lambda m: (m, 0, 0))
    sizes = [top - low for low, top in zip(bounds[:-1], bounds[1:])]
    *chunks, mine = pl.pallas_call(
        functools.partial(own_kernel, bounds),
        grid=(modules,),
        in_specs=[
            pl.BlockSpec((n, size), lambda m: (0, m)),
            small,
            small,
            pl.BlockSpec((examples, size), lambda m: (0, m)),
        ],
        out_specs=[pl.BlockSpec((groups, c, size), lambda m: (0, 0, m)) for c in sizes]
        + [pl.BlockSpec((groups, n // groups, examples), lambda m: (0, 0, 0))],
        out_shape=[jax.ShapeDtypeStruct((groups, c, dims), jnp.bfloat16) for c in sizes]
        + [jax.ShapeDtypeStruct((groups, n // groups, examples), jnp.float32)],
        scratch_shapes=[
            pltpu.VMEM((side, side // LOW, LOW, n), jnp.float32),
            pltpu.VMEM((side, side // LOW, LOW, n), jnp.float32),
            pltpu.VMEM((n, size), jnp.bfloat16),
        ],
        compiler_params=pltpu.CompilerParams(vmem_limit_bytes=VMEM),
        name="own",
    )(queries, inv_in, inv_out, store)
    return chunks, mine


def visit_raw_kernel(count, *refs):
    pieces = refs[:count]
    in_ref, out_ref, slab_ref, _, scores_ref, turned, left, held = refs[count:]
    _, groups, rows, _ = scores_ref.shape
    at = 0
    for piece in pieces:
        n = piece.shape[0] * piece.shape[1]
        held[at : at + n] = piece[...].reshape(n, piece.shape[2])
        at += n
    blocks = precondition(held[...], in_ref[0], out_ref[0], turned, left)
    for index, block in enumerate(blocks):
        held[:, index * WIDE : (index + 1) * WIDE] = block
    add_scores(held[...], slab_ref[...], scores_ref)


def visit_raw(raw, inv_in, inv_out, store, word):
    modules, side, _ = inv_in.shape
    size = side * side
    examples = store.shape[0]
    pieces = [upper for upper, _ in raw] + [lower for _, lower in raw]
    groups = pieces[0].shape[0]
    counts = [upper.shape[1] for upper, _ in raw]
    n = 2 * groups * sum(counts)
    small = pl.BlockSpec((1, side, side), lambda m: (m, 0, 0))
    scores = pl.pallas_call(
        functools.partial(visit_raw_kernel, len(pieces)),
        grid=(modules,),
        in_specs=[pl.BlockSpec((*p.shape[:2], size), lambda m: (0, 0, m)) for p in pieces]
        + [small, small, pl.BlockSpec((examples, size), lambda m: (0, m))]
        + [pl.BlockSpec(memory_space=pl.ANY)],
        out_specs=pl.BlockSpec((2, groups, sum(counts), examples), lambda m: (0, 0, 0, 0)),
        out_shape=jax.ShapeDtypeStruct((2, groups, sum(counts), examples), jnp.float32),
        scratch_shapes=[
            pltpu.VMEM((side, side // LOW, LOW, n), jnp.float32),
            pltpu.VMEM((side, side // LOW, LOW, n), jnp.float32),
            pltpu.VMEM((n, size), jnp.bfloat16),
        ],
        compiler_params=pltpu.CompilerParams(vmem_limit_bytes=VMEM),
        name="visit_raw",
    )(*pieces, inv_in, inv_out, store, word)
    flat = scores.reshape(2, -1, examples)
    at, found = 0, []
    for count in counts:
        found.append(flat[:, at : at + groups * count].reshape(2, groups, count, examples))
        at += groups * count
    return jnp.concatenate(found, axis=2)


def visit_kernel(count, upper_ref, lower_ref, slab_ref, *rest):
    *base, scores_ref = rest[count:]
    groups, rows, width = upper_ref.shape
    both = jnp.concatenate(
        [upper_ref[...].reshape(groups * rows, width), lower_ref[...].reshape(groups * rows, width)]
    )
    add_scores(both, slab_ref[...], scores_ref, *base)


def visit(upper, lower, store, first, unit, words, *base):
    groups, rows, width = upper.shape
    examples = store.shape[0]
    block = pl.BlockSpec((groups, rows, unit), lambda s: (0, 0, s))
    whole = pl.BlockSpec((2, groups, rows, examples), lambda s: (0, 0, 0, 0))
    return pl.pallas_call(
        functools.partial(visit_kernel, len(words)),
        grid=(width // unit,),
        in_specs=[
            block,
            block,
            pl.BlockSpec((examples, unit), lambda s: (0, s + first)),
        ]
        + [pl.BlockSpec(memory_space=pl.ANY) for _ in words]
        + [whole for _ in base],
        out_specs=whole,
        out_shape=jax.ShapeDtypeStruct((2, groups, rows, examples), jnp.float32),
        compiler_params=pltpu.CompilerParams(vmem_limit_bytes=VMEM),
        name="visit",
    )(upper, lower, store, *words, *base)


def shifted(value, axis, steps):
    count = lax.axis_size(axis)
    pairs = [(source, (source + steps) % count) for source in range(count)]
    return lax.ppermute(value, axis, pairs)


def grp_sum(part, dim):
    groups = lax.axis_size("grp")
    me = lax.axis_index("grp")
    total = lax.dynamic_index_in_dim(part, me, dim, keepdims=False)
    for turn in range(1, groups):
        share = lax.dynamic_index_in_dim(part, (me + turn) % groups, dim, keepdims=False)
        total = total + shifted(share, "grp", turn)
    return total


def to_owner(part, steps):
    ex = lax.axis_size("ex")
    groups = lax.axis_size("grp")
    me = lax.axis_index("grp")
    total = None
    for turn in range(groups):
        share = lax.dynamic_index_in_dim(part, (me + turn) % groups, 0, keepdims=False)
        pairs = [
            (b * groups + g, ((b + steps) % ex) * groups + (g + turn) % groups)
            for b in range(ex)
            for g in range(groups)
        ]
        arrived = lax.ppermute(share, ("ex", "grp"), pairs)
        total = arrived if total is None else total + arrived
    return total


def body(queries, inv_in, inv_out, store, listed):
    groups = lax.axis_size("grp")
    rows = queries.shape[0] // groups
    dims = queries.shape[1]
    unit = dims // sum(PIECES)
    bounds = [0]
    for part in CHUNKS:
        bounds.append(bounds[-1] + rows * part // sum(CHUNKS))
    together = lax.optimization_barrier

    def send(value):
        return shifted(value, "ex", -1), shifted(value, "ex", 1)

    split = queries.reshape(groups, rows, dims)
    first, queries = together((split[:, : bounds[1]], queries))
    came_raw = send(first)
    (a, c), mine = own(queries, inv_in, inv_out, store, groups, bounds[1:])
    cuts = []
    start = 0
    for count in PIECES:
        cuts.append(c[..., start * unit : (start + count) * unit])
        start += count

    def both_there(came, work):
        word, came, work = together((came[0][0, :, :LANES], came, work))
        pairs = [(i, i ^ 1) for i in range(lax.axis_size("ex"))]
        return lax.ppermute(word, "ex", pairs), came, work

    word, came_raw, (mine, cuts) = both_there(came_raw, (mine, cuts))
    a, cut, word = together((a, cuts[0], word))
    came_a = send(a)
    came_c = [send(cut)]
    scores_raw = visit_raw([came_raw], inv_in, inv_out, store, word)
    own_scores = grp_sum(mine, 0)
    word, came_a, (scores_raw, own_scores) = both_there(came_a, (scores_raw, own_scores))
    cut, word = together((cuts[1], word))
    came_c.append(send(cut))
    scores_a = visit(*came_a, store, 0, unit, [word])
    both = grp_sum(jnp.concatenate([scores_raw, scores_a], axis=2), 1)
    word, came_c[0], both = both_there(came_c[0], both)
    cut, word = together((cuts[2], word))
    came_c.append(send(cut))
    part = visit(*came_c[0], store, 0, unit, [word])
    both, came_c[1], part = together((both, came_c[1], part))
    both = both.astype(jnp.bfloat16)
    returned = shifted(both[0], "ex", 1), shifted(both[1], "ex", -1)
    part = visit(*came_c[1], store, PIECES[0], unit, [word], part)
    part = visit(*came_c[2], store, PIECES[0] + PIECES[1], unit, returned, part)
    upper_scores = [returned[0].astype(jnp.float32), to_owner(part[0], 1)]
    lower_scores = [returned[1].astype(jnp.float32), to_owner(part[1], -1)]

    scores = jnp.stack(
        [jnp.concatenate(upper_scores), own_scores, jnp.concatenate(lower_scores)]
    )
    return scores * mask(listed, rows, scores.shape[2])


def mask(listed, rows, examples):
    blocks = examples // SUB
    full = jnp.repeat(listed.astype(jnp.float32), QB, axis=0)
    start = lax.axis_index("grp") * rows
    mine = lax.dynamic_slice_in_dim(full, start, rows, 0)
    mine = mine.reshape(rows, 3, blocks).transpose(1, 0, 2)
    return jnp.repeat(mine, SUB, axis=2)


def solution(mesh):
    in_specs = (
        P("ex", "grp"),
        P("grp", None, None),
        P("grp", None, None),
        P("ex", "grp"),
        P("ex", None),
    )
    out_specs = P(None, ("ex", "grp"), None)
    return jax.shard_map(body, mesh=mesh, in_specs=in_specs, out_specs=out_specs, check_vma=False)
```
